32 devices in a mesh: groups: 2 (over y), space: 4 (over x, core), contour: 4 (over z).
Axes of the slice: x: 2, y: 2, z: 4, core: 2. Of those that a mesh axis runs over, the one named last changes fastest.
Arguments:
- body_force: float32 [6, 16, 1024], P('groups', 'space'), parts along dimension 0, may hold values from -6 to 6
- ice_thickness: float32 [2048], P('groups'), parts along dimension 0, may hold values from 0.5 to 4
- ice_mask: int32 [2048], P('groups'), parts along dimension 0, may hold values 0 or 1
- layer_ids: int32 [16, 1024], P('space'), may hold values from 0 to 3
- shear_modulus: float32 [4], replicated, may hold values from 0.5 to 4
- relax_rate: float32 [4], replicated, may hold values from 0.2 to 5
- node_ids: int32 [12], P('contour'), may hold values from 0 to 11, each once
- time_ids: int32 [24], P('groups'), parts along dimension 0, may hold values from 0 to 63
Outputs:
- laplace_field: float32 [24, 6, 16, 1024], P(('groups', 'contour'), None, 'space'), parts along dimension 0
- surface_motion: float32 [24, 3, 1024], P('groups', None, ('space', 'contour')), parts along dimension 0
The draws below stay inside these ranges and needn't reach their ends.
There are 2 independent parts, one for each index of `groups`. The reference program is written for one: setup_inputs(seed, part) draws one part's arguments, and reference() takes and returns one part's arrays. A program takes and returns all parts, laid end to end along the dimension named above; an argument that names none is the same for every part. Nothing has to cross between parts.
Inputs may be any that keep to these rules, and one draw needn't show every extreme that they name: `node_ids`: every contour node appears in exactly one slot.
All inputs are finite; a program needn't handle non-finite values.
Results may differ from the reference program's by a relative error of at most 0.00007.
Values sent between devices are 32-bit elements; how exact they have to be, the bound alone decides.
A program may use at most 64 MiB of HBM per device.

```python
import math
import jax
import jax.numpy as jnp
from jax import lax

HX = 128
HY = 8
TIMES = 12
T_STEPS = 64
LAYERS = 4
COARSE_SWEEPS = 8
NODES = 12
NZ = 16


def set_ends(entries, stream_key, least, largest):
    spot = [jax.random.randint(jax.random.fold_in(stream_key, axis), (), 0, length) for axis, length in enumerate(entries.shape)]
    longest = entries.shape.index(max(entries.shape))
    neighbour = spot[:longest] + [(spot[longest] + 1) % entries.shape[longest]] + spot[longest + 1:]
    return entries.at[tuple(spot)].set(least).at[tuple(neighbour)].set(largest)


def with_spikes(entries, own_key, source, target, parts, factor):
    def block_of(position):
        return (jnp.arange(entries.shape[position]) // (entries.shape[position] // parts)).reshape((-1,) + (1,) * (entries.ndim - 1 - position))

    first = jax.random.permutation(own_key, parts)[block_of(target)]
    other_side = (block_of(target) + parts // 2) % parts
    return jnp.where((block_of(source) == first) | (block_of(source) == other_side), factor * entries, entries)


def shard_levels(rng, shape, shards, least, top_value):
    def one(axis_at, shards_of):
        draws = jax.random.uniform(jax.random.fold_in(jax.random.fold_in(rng, 6), axis_at), (shards_of,), jnp.float32, least / len(shards), top_value / len(shards))
        return jnp.repeat(jnp.exp(draws), shape[axis_at] // shards_of).reshape((-1,) + (1,) * (len(shape) - axis_at - 1))

    level = one(*shards[0])
    for cut in shards[1:]:
        level = level * one(*cut)
    return level


def bell_draw_with(rng, extent, width, reach, cuts, heavy, kind=jnp.bfloat16):
    result = width * jax.random.normal(rng, extent, jnp.float32)
    if cuts:
        result = result * shard_levels(rng, extent, cuts, -0.22, 0.18)
    return jnp.clip(with_spikes(result, jax.random.fold_in(rng, 3), *heavy), -reach, reach).astype(kind)


def setup_inputs(seed: int = 0, part: int = 0) -> dict:
    streams_of = jax.random.split(jax.random.key(seed), 9)
    own_keys = jax.random.split(jax.random.fold_in(streams_of[8], part), 9)
    return {
        "body_force": bell_draw_with(own_keys[0], (3, NZ, HY * HX), 1.0, 6.0, ((1, 4),), (1, 2, 4, 2.0), jnp.float32),
        "ice_thickness": jnp.clip(jnp.exp(jax.random.uniform(own_keys[1], (HY * HX,), jnp.float32, math.log(0.5), math.log(4.0))), 0.5, 4.0),
        "ice_mask": set_ends((jax.random.randint(own_keys[2], (HY * HX,), 0, 2) < 1).astype(jnp.int32), jax.random.fold_in(own_keys[2], 1), 0, 1),
        "layer_ids": set_ends(jax.random.randint(streams_of[3], (NZ, HY * HX), 0, LAYERS), jax.random.fold_in(streams_of[3], 1), 0, LAYERS - 1).astype(jnp.int32),
        "shear_modulus": jnp.clip(jnp.exp(jax.random.uniform(streams_of[4], (LAYERS,), jnp.float32, math.log(0.5), math.log(4.0))), 0.5, 4.0),
        "relax_rate": jnp.clip(jnp.exp(jax.random.uniform(streams_of[5], (LAYERS,), jnp.float32, math.log(0.2), math.log(5.0))), 0.2, 5.0),
        "node_ids": jax.random.permutation(streams_of[6], NODES).astype(jnp.int32),
        "time_ids": set_ends(jax.random.randint(own_keys[7], (TIMES,), 0, T_STEPS), jax.random.fold_in(own_keys[7], 1), 0, T_STEPS - 1).astype(jnp.int32),
    }


OMEGA = 0.7
KAPPA = 1.0

def contour_nodes(node_ids, node_count):
    angles = -math.pi + (node_ids.astype(jnp.float32) + 0.5) * (2.0 * math.pi / node_count)
    contour_scale = 0.5 * node_count
    sine_theta = jnp.sin(angles)
    cotangent = jnp.cos(angles) / sine_theta
    pole_real = contour_scale * (0.5017 * angles * cotangent - 0.4622)
    pole_imag = contour_scale * 0.2645 * angles
    slope_real = contour_scale * 0.5017 * (cotangent - angles / (sine_theta * sine_theta))
    weight_real = contour_scale * 0.2645 / node_count + 0.0 * angles
    weight_imag = -slope_real / node_count
    return (pole_real, pole_imag, weight_real, weight_imag)

def layer_tables(pole_real, pole_imag, shear_modulus, relax_rate):
    pole_r = pole_real[:, None]
    pole_i = pole_imag[:, None]
    shifted_real = pole_r + relax_rate[None, :]
    denominator = shifted_real * shifted_real + pole_i * pole_i
    ratio_real = (pole_r * shifted_real + pole_i * pole_i) / denominator
    ratio_imag = (pole_i * shifted_real - pole_r * pole_i) / denominator
    shear_real = shear_modulus[None, :] * ratio_real
    shear_imag = shear_modulus[None, :] * ratio_imag
    shear_size = shear_modulus[None, :] * jnp.sqrt((pole_r * pole_r + pole_i * pole_i) / denominator)
    return (shear_real, shear_imag, shear_size)

def per_cell(tables, layer_ids):
    summed = jnp.zeros((tables.shape[0], 1) + layer_ids.shape, tables.dtype)
    for layer_index in range(tables.shape[1]):
        chosen = layer_ids == layer_index
        summed = summed + jnp.where(chosen[None, None], tables[:, layer_index, None, None, None], 0.0)
    return summed

def horizontal(values, row_width):
    last_size = values.shape[-1]
    column = jnp.arange(last_size) % row_width
    zero_column = jnp.zeros_like(values[..., :1])
    zero_rows = jnp.zeros_like(values[..., :row_width])
    from_left = jnp.where(column > 0, jnp.concatenate([zero_column, values[..., :-1]], axis=-1), 0.0)
    from_right = jnp.where(column < row_width - 1, jnp.concatenate([values[..., 1:], zero_column], axis=-1), 0.0)
    from_front = jnp.concatenate([zero_rows, values[..., :-row_width]], axis=-1)
    from_back = jnp.concatenate([values[..., row_width:], zero_rows], axis=-1)
    return from_left + from_right + from_front + from_back

def zero_pad(values):
    zero_layer = jnp.zeros_like(values[..., :1, :])
    return jnp.concatenate([zero_layer, values, zero_layer], axis=-2)

def operate(padded, shear_real, shear_imag, spacing_factor, row_width):
    center = padded[..., 1:-1, :]
    laplace_term = (6.0 * center - padded[..., :-2, :] - padded[..., 2:, :] - horizontal(center, row_width)) * spacing_factor
    lap_real = laplace_term[..., :3, :, :]
    lap_imag = laplace_term[..., 3:, :, :]
    out_real = shear_real * lap_real - shear_imag * lap_imag + KAPPA * center[..., :3, :, :]
    out_imag = shear_real * lap_imag + shear_imag * lap_real + KAPPA * center[..., 3:, :, :]
    return jnp.concatenate([out_real, out_imag], axis=-3)

def complex_scale(gain_real, gain_imag, values):
    val_real = values[..., :3, :, :]
    val_imag = values[..., 3:, :, :]
    return jnp.concatenate([gain_real * val_real - gain_imag * val_imag, gain_real * val_imag + gain_imag * val_real], axis=-3)

def gains(shear_real, shear_imag, shear_size, stencil_factor):
    diagonal_real = stencil_factor * shear_real + KAPPA
    diagonal_imag = stencil_factor * shear_imag
    bound_value = stencil_factor * shear_size + KAPPA
    inverse = OMEGA / (bound_value * bound_value)
    return (diagonal_real * inverse, -diagonal_imag * inverse)

def restrict(values, row_width):
    column_pairs = values[..., 0::2] + values[..., 1::2]
    half_width = row_width // 2
    shaped = column_pairs.reshape(column_pairs.shape[:-1] + (column_pairs.shape[-1] // row_width, row_width))
    row_pairs = shaped[..., :half_width] + shaped[..., half_width:]
    flat_cells = row_pairs.reshape(row_pairs.shape[:-2] + (-1,))
    depth_pairs = flat_cells.reshape(flat_cells.shape[:-2] + (flat_cells.shape[-2] // 2, 2, flat_cells.shape[-1]))
    return (depth_pairs[..., 0, :] + depth_pairs[..., 1, :]) * 0.125

def prolong(values, row_width):
    wide_copy = jnp.repeat(values, 2, axis=-1)
    shaped = wide_copy.reshape(wide_copy.shape[:-1] + (wide_copy.shape[-1] // row_width, row_width))
    tall_copy = jnp.concatenate([shaped, shaped], axis=-1)
    flat_cells = tall_copy.reshape(tall_copy.shape[:-2] + (-1,))
    return jnp.repeat(flat_cells, 2, axis=-2)

def solve_node(forcing, shear_real, shear_imag, shear_size, row_width):
    gain_real, gain_imag = gains(shear_real, shear_imag, shear_size, 6.0)

    def residual(field):
        return forcing - operate(zero_pad(field), shear_real, shear_imag, 1.0, row_width)
    field = complex_scale(gain_real, gain_imag, forcing)
    field = field + complex_scale(gain_real, gain_imag, residual(field))
    coarse_rhs = restrict(residual(field), row_width)
    coarse_real = restrict(shear_real, row_width)
    coarse_imag = restrict(shear_imag, row_width)
    coarse_size = restrict(shear_size, row_width)
    coarse_gr, coarse_gi = gains(coarse_real, coarse_imag, coarse_size, 1.5)
    half_width = row_width // 2
    correction = complex_scale(coarse_gr, coarse_gi, coarse_rhs)
    for counter in range(COARSE_SWEEPS - 1):
        correction = correction + complex_scale(coarse_gr, coarse_gi, coarse_rhs - operate(zero_pad(correction), coarse_real, coarse_imag, 0.25, half_width))
    leftover = coarse_rhs - operate(zero_pad(correction), coarse_real, coarse_imag, 0.25, half_width)
    correction = correction + lax.optimization_barrier(jnp.mean(leftover, axis=-2, keepdims=True)) / KAPPA
    field = field + prolong(correction, row_width)
    for counter in range(2):
        field = field + complex_scale(gain_real, gain_imag, residual(field))
    return field

def reference(body_force, ice_thickness, ice_mask, layer_ids, shear_modulus, relax_rate, node_ids, time_ids):
    pole_real, pole_imag, weight_real, weight_imag = contour_nodes(node_ids, NODES)
    tables = layer_tables(pole_real, pole_imag, shear_modulus, relax_rate)
    cell_real = per_cell(tables[0], layer_ids)
    cell_imag = per_cell(tables[1], layer_ids)
    cell_size = per_cell(tables[2], layer_ids)
    ice_load = -ice_thickness * ice_mask.astype(jnp.float32)
    forcing_base = body_force.at[0, 0, :].add(ice_load)
    pole_square = pole_real * pole_real + pole_imag * pole_imag
    inverse_real = pole_real / pole_square
    inverse_imag = -pole_imag / pole_square

    def one_node(node_items):
        inv_r, inv_i, node_real, node_imag, node_size = node_items
        forcing = jnp.concatenate([forcing_base * inv_r, forcing_base * inv_i], axis=0)
        return solve_node(forcing, node_real, node_imag, node_size, HX)
    fields = lax.map(one_node, (inverse_real, inverse_imag, cell_real, cell_imag, cell_size))
    time_values = (time_ids.astype(jnp.float32) + 1.0) * (2.0 / T_STEPS)
    growth = jnp.exp(time_values[:, None] * pole_real[None, :])
    phase_angle = time_values[:, None] * pole_imag[None, :]
    factor_real = growth * (weight_real[None, :] * jnp.cos(phase_angle) - weight_imag[None, :] * jnp.sin(phase_angle))
    factor_imag = growth * (weight_real[None, :] * jnp.sin(phase_angle) + weight_imag[None, :] * jnp.cos(phase_angle))
    top_layer = fields[:, :, 0, :]
    surface_motion = jnp.einsum('jk,kcs->jcs', factor_real, top_layer[:, :3], precision=lax.Precision.HIGHEST) - jnp.einsum('jk,kcs->jcs', factor_imag, top_layer[:, 3:], precision=lax.Precision.HIGHEST)
    return (fields, surface_motion)
```

```python
import functools
import math

import jax
import jax.numpy as jnp
from jax import lax
from jax.experimental import pallas as pl
from jax.experimental.pallas import tpu as pltpu
from jax.sharding import PartitionSpec as P

HX = 128
HY = 8
T_STEPS = 64
COARSE_SWEEPS = 8
OMEGA = 0.7
MESH = pl.DeviceIdType.MESH
F32 = jnp.float32


def poles(nodes, node_count):
    angles = -math.pi + (nodes + 0.5) * (2.0 * math.pi / node_count)
    scale = 0.5 * node_count
    sine = jnp.sin(angles)
    cot = jnp.cos(angles) / sine
    pole_r = scale * (0.5017 * angles * cot - 0.4622)
    pole_i = scale * 0.2645 * angles
    slope_r = scale * 0.5017 * (cot - angles / (sine * sine))
    weight_r = scale * 0.2645 / node_count
    weight_i = -slope_r / node_count
    return pole_r, pole_i, weight_r, weight_i


def iota(shape, axis):
    return lax.broadcasted_iota(jnp.int32, shape, len(shape) + axis)


def shift(v, lanes, rows):
    if lanes:
        v = pltpu.roll(v, lanes % HX, v.ndim - 1)
    if rows:
        v = pltpu.roll(v, rows % HY, v.ndim - 2)
    return v


def sides(v, step):
    lane, row = iota(v.shape, -1), iota(v.shape, -2)
    left = jnp.where(lane >= step, shift(v, step, 0), 0.0)
    right = jnp.where(lane < HX - step, shift(v, -step, 0), 0.0)
    front = jnp.where(row >= step, shift(v, 0, step), 0.0)
    back = jnp.where(row < HY - step, shift(v, 0, -step), 0.0)
    return (left + right) + (front + back)


def even_lane(shape):
    return iota(shape, -1) % 2 == 0


def even_row(shape):
    return iota(shape, -2) % 2 == 0


def partner_lane(v):
    return jnp.where(even_lane(v.shape), shift(v, -1, 0), shift(v, 1, 0))


def partner_row(v):
    return jnp.where(even_row(v.shape), shift(v, 0, -1), shift(v, 0, 1))


def pack(a0, a1, a2, a3):
    el, er = even_lane(a0.shape), even_row(a0.shape)
    h0 = jnp.where(el, a0, a1) + jnp.where(el, shift(a0, -1, 0), shift(a1, 1, 0))
    h1 = jnp.where(el, a2, a3) + jnp.where(el, shift(a2, -1, 0), shift(a3, 1, 0))
    return jnp.where(er, h0, h1) + jnp.where(er, shift(h0, 0, -1), shift(h1, 0, 1))


def next_slot(v):
    return jnp.where(
        even_lane(v.shape),
        shift(v, -1, 0),
        jnp.where(even_row(v.shape), shift(v, 1, -1), 0.0),
    )


def last_slot(v):
    return jnp.where(
        even_lane(v.shape),
        jnp.where(even_row(v.shape), 0.0, shift(v, -1, 1)),
        shift(v, 1, 0),
    )


def prolong(v, slot):
    v = jnp.where(iota(v.shape, -1) % 2 == slot % 2, v, partner_lane(v))
    return jnp.where(iota(v.shape, -2) % 2 == slot // 2, v, partner_row(v))


def scaled(real, imag, v):
    re, im = v[:3], v[3:]
    return jnp.concatenate([real * re - imag * im, real * im + imag * re], axis=0)


def kernel(
    S, C, NS, L, D, NT, W,
    body_ref, thick_ref, mask_ref, layer_ref, shear_ref, relax_ref, node_ref, time_ref,
    field_ref, surf_ref,
    body_all, layer_all, tab, inv, coef, base, u1, u2, cnt, rz, coarse, top, sbuf, rbuf,
    body_send, body_recv, layer_send, layer_recv, surf_send, surf_recv,
):
    NZ = S * D
    NCZ = NZ // 2
    NJ = NCZ // 4
    NTP = sbuf.shape[2]
    R = sbuf.shape[0]
    tile = (HY, HX)
    me_s = lax.axis_index("space")
    me_c = lax.axis_index("contour")

    barrier = pltpu.get_barrier_semaphore()
    for k in range(1, S):
        pl.semaphore_signal(
            barrier, inc=1, device_id={"space": lax.rem(me_s + k, S)}, device_id_type=MESH
        )
    for k in range(1, C):
        pl.semaphore_signal(
            barrier, inc=1, device_id={"contour": lax.rem(me_c + k, C)}, device_id_type=MESH
        )
    pl.semaphore_wait(barrier, S + C - 2)

    def slab_copies(k):
        peer = {"space": lax.rem(me_s + k, S)}
        return (
            pltpu.make_async_remote_copy(
                layer_ref, layer_all.at[me_s], layer_send.at[k], layer_recv.at[k],
                device_id=peer, device_id_type=MESH,
            ),
            pltpu.make_async_remote_copy(
                body_ref, body_all.at[me_s], body_send.at[k], body_recv.at[k],
                device_id=peer, device_id_type=MESH,
            ),
        )

    sends = [slab_copies(k) for k in range(1, S)]
    for pair in sends:
        for copy in pair:
            copy.start()

    node_vec = jnp.stack([jnp.full(tile, node_ref[n].astype(F32)) for n in range(NS)])
    pole_r, pole_i, weight_r, weight_i = poles(node_vec, NS * C)
    square = pole_r * pole_r + pole_i * pole_i
    inv_r, inv_i = pole_r / square, -pole_i / square
    for n in range(NS):
        inv[n, 0] = inv_r[n]
        inv[n, 1] = inv_i[n]
    for l in range(L):
        shear, relax = shear_ref[l], relax_ref[l]
        moved = pole_r + relax
        denom = moved * moved + pole_i * pole_i
        mu_r = shear * ((pole_r * moved + pole_i * pole_i) / denom)
        mu_i = shear * ((pole_i * moved - pole_r * pole_i) / denom)
        size = shear * jnp.sqrt(square / denom)
        diag_r, diag_i = 6.0 * mu_r + 1.0, 6.0 * mu_i
        bound = 6.0 * size + 1.0
        scale = OMEGA / (bound * bound)
        gain_r, gain_i = diag_r * scale, -diag_i * scale
        rows = (
            1.0 - scale * (diag_r * diag_r + diag_i * diag_i),
            gain_r * mu_r - gain_i * mu_i,
            gain_r * mu_i + gain_i * mu_r,
            gain_r * inv_r - gain_i * inv_i,
            gain_r * inv_i + gain_i * inv_r,
            mu_r,
            mu_i,
            size,
        )
        for q, value in enumerate(rows):
            for n in range(NS):
                tab[n, l, q] = value[n]

    spots = iota((NTP, HX), -2)
    times = jnp.zeros((NTP, HX), F32)
    for j in range(NT):
        times = jnp.where(spots == j, (time_ref[j].astype(F32) + 1.0) * (2.0 / T_STEPS), times)
    factors = []
    for n in range(NS):
        growth = jnp.exp(times * pole_r[n, :1, :])
        phase = times * pole_i[n, :1, :]
        cosine, sine = jnp.cos(phase), jnp.sin(phase)
        wi = weight_i[n, :1, :]
        factors.append(
            (growth * (weight_r * cosine - wi * sine), growth * (weight_r * sine + wi * cosine))
        )

    blank = jnp.zeros((NS, 2, 6) + tile, F32)
    for u in (u1, u2):
        u[:, pl.ds(0, 2)] = blank
        u[:, pl.ds(NZ + 2, 2)] = blank

    body_all[me_s] = body_ref[...]
    layer_all[me_s] = layer_ref[...]
    ice = thick_ref[...] * mask_ref[...].astype(F32)

    def take_slab(slab):
        for zp in range(D // 2):
            counts = None
            for z in (2 * zp, 2 * zp + 1):
                at = slab * D + z
                ids = layer_all[slab, pl.ds(z, HY, stride=D), :]
                force = jnp.stack(
                    [body_all[slab, c, pl.ds(z, HY, stride=D), :] for c in range(3)]
                )
                if z == 0:
                    load = jnp.where(slab == 0, ice, jnp.zeros_like(ice))
                    force = jnp.concatenate([(force[0] - load)[None], force[1:]], axis=0)
                base[at] = force
                one = [jnp.where(ids == l, 1.0, 0.0) for l in range(1, L)]
                counts = one if counts is None else [a + b for a, b in zip(counts, one)]
                wide = jnp.broadcast_to(ids[None], (7,) + tile)
                for n in range(NS):
                    value = tab[n, 0, pl.ds(0, 7)]
                    for l in range(1, L):
                        value = jnp.where(wide == l, tab[n, l, pl.ds(0, 7)], value)
                    coef[n, at] = value
                    u1[n, at + 2] = jnp.concatenate(
                        [value[3][None] * force, value[4][None] * force], axis=0
                    )
            for l in range(L - 1):
                cnt[slab * (D // 2) + zp, l] = counts[l]

    take_slab(me_s)

    def arrive(k, carry):
        for copy in slab_copies(k):
            copy.wait_recv()
        take_slab(lax.rem(me_s - k + S, S))
        return carry

    lax.fori_loop(1, S, arrive, 0)

    def sweep(n, at, v, below, above):
        co = coef[n, at]
        around = below + above + sides(v, 1)
        return u1[n, at + 2] + co[0][None] * v + scaled(co[1][None], co[2][None], around)

    def second(i, carry):
        n, z = i // NZ, i % NZ
        u2[n, z + 2] = sweep(n, z, u1[n, z + 2], u1[n, z + 1], u1[n, z + 3])
        return carry

    lax.fori_loop(0, NS * NZ, second, 0, unroll=2)

    def residual(i, carry):
        n, zc = i // NCZ, i % NCZ
        total = None
        for z in (2 * zc, 2 * zc + 1):
            mu_r, mu_i = coef[n, z, 5][None], coef[n, z, 6][None]
            force = base[z]
            v = u2[n, z + 2]
            lap = u2[n, z + 1] + u2[n, z + 3] + sides(v, 1) - 6.0 * v
            right = jnp.concatenate([inv[n, 0][None] * force, inv[n, 1][None] * force], axis=0)
            r = right - v + scaled(mu_r, mu_i, lap)
            total = r if total is None else total + r
        rz[n, zc] = total
        return carry

    lax.fori_loop(0, NS * NCZ, residual, 0)

    counts = [pack(*[cnt[q * NJ + j] for q in range(4)]) * 0.125 for j in range(NJ)]

    def solve(n, carry):
        rhs, first, dd, hr, hi, mr, mi = [], [], [], [], [], [], []
        for j in range(NJ):
            share = [counts[j][l] for l in range(L - 1)]
            rest = 1.0 - sum(share[1:], share[0])
            mixed = []
            for q in (5, 6, 7):
                value = rest * tab[n, 0, q]
                for l in range(1, L):
                    value = value + share[l - 1] * tab[n, l, q]
                mixed.append(value)
            mu_r, mu_i, size = mixed
            diag_r, diag_i = 1.5 * mu_r + 1.0, 1.5 * mu_i
            bound = 1.5 * size + 1.0
            scale = OMEGA / (bound * bound)
            gain_r, gain_i = diag_r * scale, -diag_i * scale
            mu_r, mu_i = 0.25 * mu_r, 0.25 * mu_i
            b = pack(*[rz[n, q * NJ + j] for q in range(4)]) * 0.125
            rhs.append(b)
            first.append(scaled(gain_r[None], gain_i[None], b))
            dd.append((1.0 - scale * (diag_r * diag_r + diag_i * diag_i))[None])
            hr.append((gain_r * mu_r - gain_i * mu_i)[None])
            hi.append((gain_r * mu_i + gain_i * mu_r)[None])
            mr.append(mu_r[None])
            mi.append(mu_i[None])

        def around(e):
            out = []
            for j in range(NJ):
                above = e[j + 1] if j < NJ - 1 else next_slot(e[0])
                below = e[j - 1] if j > 0 else last_slot(e[NJ - 1])
                out.append(above + below + sides(e[j], 2))
            return out

        def step(counter, e):
            near = around(e)
            return tuple(
                first[j] + dd[j] * e[j] + scaled(hr[j], hi[j], near[j]) for j in range(NJ)
            )

        e = lax.fori_loop(0, COARSE_SWEEPS - 1, step, tuple(first))
        near = around(e)
        left = None
        for j in range(NJ):
            part = rhs[j] - e[j] + scaled(mr[j], mi[j], near[j] - 6.0 * e[j])
            left = part if left is None else left + part
        left = left + partner_lane(left)
        left = (left + partner_row(left)) * (1.0 / NCZ)
        for j in range(NJ):
            coarse[n, j] = e[j] + left
        return carry

    lax.fori_loop(0, NS, solve, 0)

    def window(n, start, reach_up, count):
        lo = -2 if reach_up else 0
        third = {}
        for z in range(lo, count + 2, 2):
            zc = start // 2 + z // 2
            inside = jnp.where((zc >= 0) & (zc < NCZ), 1.0, 0.0)
            at = jnp.clip(zc, 0, NCZ - 1)
            e = prolong(coarse[n, at % NJ], at // NJ) * inside
            for zz in (z, z + 1):
                if zz < count + 2:
                    third[zz] = u2[n, start + zz + 2] + e
        zero = jnp.zeros((6,) + tile, F32)
        fourth = {}
        for z in range(max(lo + 1, lo if reach_up else 0) if reach_up else 0, count + 1):
            at = start + z
            inside = jnp.where((at >= 0) & (at < NZ), 1.0, 0.0)
            value = sweep(n, jnp.clip(at, 0, NZ - 1), third[z], third.get(z - 1, zero), third[z + 1])
            fourth[z] = value * inside
        return [
            sweep(n, start + z, fourth[z], fourth.get(z - 1, zero), fourth[z + 1])
            for z in range(count)
        ]

    def surface(n, carry):
        top[n] = window(n, jnp.int32(0), False, 1)[0]
        return carry

    lax.fori_loop(0, NS, surface, 0)

    row0 = (me_s * (C * W)) // HX
    for r in range(R):
        for c in range(3):
            total = None
            for n in range(NS):
                re = top[n, c, pl.ds(row0 + r, 1), :]
                im = top[n, c + 3, pl.ds(row0 + r, 1), :]
                part = factors[n][0] * re - factors[n][1] * im
                total = part if total is None else total + part
            sbuf[r, c] = total

    def surf_copy(k):
        to = lax.rem(me_c + k, C)
        return pltpu.make_async_remote_copy(
            sbuf.at[(to * W) // HX if R > 1 else 0], rbuf.at[k - 1],
            surf_send.at[k], surf_recv.at[k],
            device_id={"contour": to}, device_id_type=MESH,
        )

    surf_sends = [surf_copy(k) for k in range(1, C)]
    for copy in surf_sends:
        copy.start()

    def finish(n, carry):
        for z, value in enumerate(window(n, me_s * D, True, D)):
            for c in range(6):
                field_ref[n, c, pl.ds(z, HY, stride=D), :] = value[c]
        return carry

    lax.fori_loop(0, NS, finish, 0)

    for copy in surf_sends:
        copy.wait_recv()
    total = sbuf[(me_c * W) // HX if R > 1 else 0]
    for k in range(1, C):
        total = total + rbuf[k - 1]
    offset = lax.rem((me_s * C + me_c) * W, HX)
    surf_ref[...] = pltpu.roll(total, lax.rem(HX - offset, HX), 2)

    for copy in surf_sends:
        copy.wait_send()
    for pair in sends:
        for copy in pair:
            copy.wait_send()


def per_device(
    body_force, ice_thickness, ice_mask, layer_ids, shear_modulus, relax_rate, node_ids, time_ids
):
    S, C = lax.axis_size("space"), lax.axis_size("contour")
    NS, L, D, NT = node_ids.shape[0], shear_modulus.shape[0], layer_ids.shape[0], time_ids.shape[0]
    NZ = S * D
    NCZ = NZ // 2
    NJ = NCZ // 4
    W = HX * HY // (S * C)
    R = max(1, C * W // HX)
    NTP = -(-NT // 8) * 8
    body = body_force.reshape(3, D, HY, HX).transpose(0, 2, 1, 3).reshape(3, HY * D, HX)
    layers = layer_ids.reshape(D, HY, HX).transpose(1, 0, 2).reshape(HY * D, HX)
    tile = (HY, HX)
    vmem = pl.BlockSpec(memory_space=pltpu.VMEM)
    smem = pl.BlockSpec(memory_space=pltpu.SMEM)
    field, surf = pl.pallas_call(
        functools.partial(kernel, S, C, NS, L, D, NT, W),
        out_shape=(
            jax.ShapeDtypeStruct((NS, 6, HY * D, HX), F32),
            jax.ShapeDtypeStruct((3, NTP, HX), F32),
        ),
        in_specs=[vmem] * 4 + [smem] * 4,
        out_specs=(vmem, vmem),
        scratch_shapes=[
            pltpu.VMEM((S, 3, HY * D, HX), F32),
            pltpu.VMEM((S, HY * D, HX), jnp.int32),
            pltpu.VMEM((NS, L, 8) + tile, F32),
            pltpu.VMEM((NS, 2) + tile, F32),
            pltpu.VMEM((NS, NZ, 7) + tile, F32),
            pltpu.VMEM((NZ, 3) + tile, F32),
            pltpu.VMEM((NS, NZ + 4, 6) + tile, F32),
            pltpu.VMEM((NS, NZ + 4, 6) + tile, F32),
            pltpu.VMEM((NCZ, L - 1) + tile, F32),
            pltpu.VMEM((NS, NCZ, 6) + tile, F32),
            pltpu.VMEM((NS, NJ, 6) + tile, F32),
            pltpu.VMEM((NS, 6) + tile, F32),
            pltpu.VMEM((R, 3, NTP, HX), F32),
            pltpu.VMEM((C - 1, 3, NTP, HX), F32),
            pltpu.SemaphoreType.DMA((S,)),
            pltpu.SemaphoreType.DMA((S,)),
            pltpu.SemaphoreType.DMA((S,)),
            pltpu.SemaphoreType.DMA((S,)),
            pltpu.SemaphoreType.DMA((C,)),
            pltpu.SemaphoreType.DMA((C,)),
        ],
        compiler_params=pltpu.CompilerParams(
            collective_id=0, has_side_effects=True, vmem_limit_bytes=48 * 1024 * 1024
        ),
    )(
        body,
        ice_thickness.reshape(HY, HX),
        ice_mask.reshape(HY, HX),
        layers,
        shear_modulus,
        relax_rate,
        node_ids,
        time_ids,
    )
    field = field.reshape(NS, 6, HY, D, HX).transpose(0, 1, 3, 2, 4).reshape(NS, 6, D, HY * HX)
    surf = surf[:, :NT, :W].transpose(1, 0, 2)
    return (field, surf)


def solution(mesh):
    in_specs = (
        P("groups", "space", None),
        P("groups"),
        P("groups"),
        P("space", None),
        P(),
        P(),
        P("contour"),
        P("groups"),
    )
    out_specs = (
        P(("groups", "contour"), None, "space", None),
        P("groups", None, ("space", "contour")),
    )
    return jax.shard_map(
        per_device, mesh=mesh, in_specs=in_specs, out_specs=out_specs, check_vma=False
    )
```

```python
import functools
import math

import jax
import jax.numpy as jnp
from jax import lax
from jax.experimental import pallas as pl
from jax.experimental.pallas import tpu as pltpu
from jax.sharding import PartitionSpec as P

HX = 128
HY = 8
T_STEPS = 64
COARSE_SWEEPS = 8
OMEGA = 0.7
MESH = pl.DeviceIdType.MESH
F32 = jnp.float32


def poles(nodes, node_count):
    angles = -math.pi + (nodes + 0.5) * (2.0 * math.pi / node_count)
    scale = 0.5 * node_count
    sine = jnp.sin(angles)
    cot = jnp.cos(angles) / sine
    pole_r = scale * (0.5017 * angles * cot - 0.4622)
    pole_i = scale * 0.2645 * angles
    slope_r = scale * 0.5017 * (cot - angles / (sine * sine))
    weight_r = scale * 0.2645 / node_count
    weight_i = -slope_r / node_count
    return pole_r, pole_i, weight_r, weight_i


def iota(shape, axis):
    return lax.broadcasted_iota(jnp.int32, shape, len(shape) + axis)


def shift(v, lanes, rows):
    if lanes:
        v = pltpu.roll(v, lanes % HX, v.ndim - 1)
    if rows:
        v = pltpu.roll(v, rows % HY, v.ndim - 2)
    return v


def sides(v, step):
    lane, row = iota(v.shape, -1), iota(v.shape, -2)
    left = jnp.where(lane >= step, shift(v, step, 0), 0.0)
    right = jnp.where(lane < HX - step, shift(v, -step, 0), 0.0)
    front = jnp.where(row >= step, shift(v, 0, step), 0.0)
    back = jnp.where(row < HY - step, shift(v, 0, -step), 0.0)
    return (left + right) + (front + back)


def even_lane(shape):
    return iota(shape, -1) % 2 == 0


def even_row(shape):
    return iota(shape, -2) % 2 == 0


def partner_lane(v):
    return jnp.where(even_lane(v.shape), shift(v, -1, 0), shift(v, 1, 0))


def partner_row(v):
    return jnp.where(even_row(v.shape), shift(v, 0, -1), shift(v, 0, 1))


def pack(a0, a1, a2, a3):
    el, er = even_lane(a0.shape), even_row(a0.shape)
    h0 = jnp.where(el, a0, a1) + jnp.where(el, shift(a0, -1, 0), shift(a1, 1, 0))
    h1 = jnp.where(el, a2, a3) + jnp.where(el, shift(a2, -1, 0), shift(a3, 1, 0))
    return jnp.where(er, h0, h1) + jnp.where(er, shift(h0, 0, -1), shift(h1, 0, 1))


def next_slot(v):
    return jnp.where(
        even_lane(v.shape),
        shift(v, -1, 0),
        jnp.where(even_row(v.shape), shift(v, 1, -1), 0.0),
    )


def last_slot(v):
    return jnp.where(
        even_lane(v.shape),
        jnp.where(even_row(v.shape), 0.0, shift(v, -1, 1)),
        shift(v, 1, 0),
    )


def prolong(v, slot):
    v = jnp.where(iota(v.shape, -1) % 2 == slot % 2, v, partner_lane(v))
    return jnp.where(iota(v.shape, -2) % 2 == slot // 2, v, partner_row(v))


def scaled(real, imag, v):
    re, im = v[:3], v[3:]
    return jnp.concatenate([real * re - imag * im, real * im + imag * re], axis=0)


def kernel(
    S, C, NS, L, D, NT, W,
    body_in, thick_in, mask_in, layer_in, shear_in, relax_in, node_in, time_in,
    field_ref, surf_ref,
    thick_ref, mask_ref, shear_ref, relax_ref, node_ref, time_ref, load_sem,
    body_all, layer_all, tab, inv, coef, base, u1, u2, cnt, rz, coarse, top, sbuf, rbuf,
    body_send, body_recv, layer_send, layer_recv, surf_send, surf_recv,
):
    NZ = S * D
    NCZ = NZ // 2
    NJ = NCZ // 4
    NTP = sbuf.shape[2]
    R = sbuf.shape[0]
    tile = (HY, HX)
    me_s = lax.axis_index("space")
    me_c = lax.axis_index("contour")

    barrier = pltpu.get_barrier_semaphore()
    for k in range(1, S):
        pl.semaphore_signal(
            barrier, inc=1, device_id={"space": lax.rem(me_s + k, S)}, device_id_type=MESH
        )
    for k in range(1, C):
        pl.semaphore_signal(
            barrier, inc=1, device_id={"contour": lax.rem(me_c + k, C)}, device_id_type=MESH
        )
    loads = [
        pltpu.make_async_copy(source, target, load_sem.at[i])
        for i, (source, target) in enumerate(
            (
                (layer_in, layer_all.at[me_s]),
                (body_in, body_all.at[me_s]),
                (node_in, node_ref),
                (shear_in, shear_ref),
                (relax_in, relax_ref),
                (time_in, time_ref),
                (thick_in, thick_ref),
                (mask_in, mask_ref),
            )
        )
    ]
    for copy in loads:
        copy.start()
    for copy in loads:
        copy.wait()
    pl.semaphore_wait(barrier, S + C - 2)

    def slab_copies(k):
        peer = {"space": lax.rem(me_s + k, S)}
        return (
            pltpu.make_async_remote_copy(
                layer_all.at[me_s], layer_all.at[me_s], layer_send.at[k], layer_recv.at[k],
                device_id=peer, device_id_type=MESH,
            ),
            pltpu.make_async_remote_copy(
                body_all.at[me_s], body_all.at[me_s], body_send.at[k], body_recv.at[k],
                device_id=peer, device_id_type=MESH,
            ),
        )

    sends = [slab_copies(k) for k in range(1, S)]
    for pair in sends:
        for copy in pair:
            copy.start()

    node_vec = jnp.stack([jnp.full(tile, node_ref[n].astype(F32)) for n in range(NS)])
    pole_r, pole_i, weight_r, weight_i = poles(node_vec, NS * C)
    square = pole_r * pole_r + pole_i * pole_i
    inv_r, inv_i = pole_r / square, -pole_i / square
    for n in range(NS):
        inv[n, 0] = inv_r[n]
        inv[n, 1] = inv_i[n]
    for l in range(L):
        shear, relax = shear_ref[l], relax_ref[l]
        moved = pole_r + relax
        denom = moved * moved + pole_i * pole_i
        mu_r = shear * ((pole_r * moved + pole_i * pole_i) / denom)
        mu_i = shear * ((pole_i * moved - pole_r * pole_i) / denom)
        size = shear * jnp.sqrt(square / denom)
        diag_r, diag_i = 6.0 * mu_r + 1.0, 6.0 * mu_i
        bound = 6.0 * size + 1.0
        scale = OMEGA / (bound * bound)
        gain_r, gain_i = diag_r * scale, -diag_i * scale
        rows = (
            1.0 - scale * (diag_r * diag_r + diag_i * diag_i),
            gain_r * mu_r - gain_i * mu_i,
            gain_r * mu_i + gain_i * mu_r,
            gain_r * inv_r - gain_i * inv_i,
            gain_r * inv_i + gain_i * inv_r,
            mu_r,
            mu_i,
            size,
        )
        for q, value in enumerate(rows):
            for n in range(NS):
                tab[n, l, q] = value[n]

    spots = iota((NTP, HX), -2)
    times = jnp.zeros((NTP, HX), F32)
    for j in range(NT):
        times = jnp.where(spots == j, (time_ref[j].astype(F32) + 1.0) * (2.0 / T_STEPS), times)
    factors = []
    for n in range(NS):
        growth = jnp.exp(times * pole_r[n, :1, :])
        phase = times * pole_i[n, :1, :]
        cosine, sine = jnp.cos(phase), jnp.sin(phase)
        wi = weight_i[n, :1, :]
        factors.append(
            (growth * (weight_r * cosine - wi * sine), growth * (weight_r * sine + wi * cosine))
        )

    blank = jnp.zeros((NS, 2, 6) + tile, F32)
    for u in (u1, u2):
        u[:, pl.ds(0, 2)] = blank
        u[:, pl.ds(NZ + 2, 2)] = blank

    ice = thick_ref[...] * mask_ref[...].astype(F32)

    def take_slab(slab):
        for zp in range(D // 2):
            counts = None
            for z in (2 * zp, 2 * zp + 1):
                at = slab * D + z
                ids = layer_all[slab, pl.ds(z, HY, stride=D), :]
                force = jnp.stack(
                    [body_all[slab, c, pl.ds(z, HY, stride=D), :] for c in range(3)]
                )
                if z == 0:
                    load = jnp.where(slab == 0, ice, jnp.zeros_like(ice))
                    force = jnp.concatenate([(force[0] - load)[None], force[1:]], axis=0)
                base[at] = force
                one = [jnp.where(ids == l, 1.0, 0.0) for l in range(1, L)]
                counts = one if counts is None else [a + b for a, b in zip(counts, one)]
                wide = jnp.broadcast_to(ids[None], (7,) + tile)
                for n in range(NS):
                    value = tab[n, 0, pl.ds(0, 7)]
                    for l in range(1, L):
                        value = jnp.where(wide == l, tab[n, l, pl.ds(0, 7)], value)
                    coef[n, at] = value
                    u1[n, at + 2] = jnp.concatenate(
                        [value[3][None] * force, value[4][None] * force], axis=0
                    )
            for l in range(L - 1):
                cnt[slab * (D // 2) + zp, l] = counts[l]

    take_slab(me_s)

    def arrive(k, carry):
        for copy in slab_copies(k):
            copy.wait_recv()
        take_slab(lax.rem(me_s - k + S, S))
        return carry

    lax.fori_loop(1, S, arrive, 0)

    def sweep(n, at, v, below, above):
        co = coef[n, at]
        around = below + above + sides(v, 1)
        return u1[n, at + 2] + co[0][None] * v + scaled(co[1][None], co[2][None], around)

    def second(z, carry):
        for n in range(NS):
            u2[n, z + 2] = sweep(n, z, u1[n, z + 2], u1[n, z + 1], u1[n, z + 3])
        return carry

    lax.fori_loop(0, NZ, second, 0, unroll=4)

    def residual(zc, carry):
        for n in range(NS):
            total = None
            for z in (2 * zc, 2 * zc + 1):
                mu_r, mu_i = coef[n, z, 5][None], coef[n, z, 6][None]
                force = base[z]
                v = u2[n, z + 2]
                lap = u2[n, z + 1] + u2[n, z + 3] + sides(v, 1) - 6.0 * v
                right = jnp.concatenate([inv[n, 0][None] * force, inv[n, 1][None] * force], axis=0)
                r = right - v + scaled(mu_r, mu_i, lap)
                total = r if total is None else total + r
            rz[n, zc] = total
        return carry

    lax.fori_loop(0, NCZ, residual, 0, unroll=2)

    counts = [pack(*[cnt[q * NJ + j] for q in range(4)]) * 0.125 for j in range(NJ)]

    def prepare(n):
        rhs, first, dd, hr, hi, mr, mi = [], [], [], [], [], [], []
        for j in range(NJ):
            share = [counts[j][l] for l in range(L - 1)]
            rest = 1.0 - sum(share[1:], share[0])
            mixed = []
            for q in (5, 6, 7):
                value = rest * tab[n, 0, q]
                for l in range(1, L):
                    value = value + share[l - 1] * tab[n, l, q]
                mixed.append(value)
            mu_r, mu_i, size = mixed
            diag_r, diag_i = 1.5 * mu_r + 1.0, 1.5 * mu_i
            bound = 1.5 * size + 1.0
            scale = OMEGA / (bound * bound)
            gain_r, gain_i = diag_r * scale, -diag_i * scale
            mu_r, mu_i = 0.25 * mu_r, 0.25 * mu_i
            b = pack(*[rz[n, q * NJ + j] for q in range(4)]) * 0.125
            rhs.append(b)
            first.append(scaled(gain_r[None], gain_i[None], b))
            dd.append((1.0 - scale * (diag_r * diag_r + diag_i * diag_i))[None])
            hr.append((gain_r * mu_r - gain_i * mu_i)[None])
            hi.append((gain_r * mu_i + gain_i * mu_r)[None])
            mr.append(mu_r[None])
            mi.append(mu_i[None])
        return rhs, first, dd, hr, hi, mr, mi

    def around(e):
        out = []
        for j in range(NJ):
            above = e[j + 1] if j < NJ - 1 else next_slot(e[0])
            below = e[j - 1] if j > 0 else last_slot(e[NJ - 1])
            out.append(above + below + sides(e[j], 2))
        return out

    plans = [prepare(n) for n in range(NS)]

    def step(counter, states):
        new = []
        for n in range(NS):
            rhs, first, dd, hr, hi, mr, mi = plans[n]
            e = states[n]
            near = around(e)
            new.append(
                tuple(first[j] + dd[j] * e[j] + scaled(hr[j], hi[j], near[j]) for j in range(NJ))
            )
        return tuple(new)

    states = lax.fori_loop(
        0, COARSE_SWEEPS - 1, step, tuple(tuple(plans[n][1]) for n in range(NS))
    )
    for n in range(NS):
        rhs, first, dd, hr, hi, mr, mi = plans[n]
        e = states[n]
        near = around(e)
        left = None
        for j in range(NJ):
            part = rhs[j] - e[j] + scaled(mr[j], mi[j], near[j] - 6.0 * e[j])
            left = part if left is None else left + part
        left = left + partner_lane(left)
        left = (left + partner_row(left)) * (1.0 / NCZ)
        for j in range(NJ):
            coarse[n, j] = e[j] + left

    def window(n, start, reach_up, count):
        lo = -2 if reach_up else 0
        third = {}
        for z in range(lo, count + 2, 2):
            zc = start // 2 + z // 2
            inside = jnp.where((zc >= 0) & (zc < NCZ), 1.0, 0.0)
            at = jnp.clip(zc, 0, NCZ - 1)
            e = prolong(coarse[n, at % NJ], at // NJ) * inside
            for zz in (z, z + 1):
                if zz < count + 2:
                    third[zz] = u2[n, start + zz + 2] + e
        zero = jnp.zeros((6,) + tile, F32)
        fourth = {}
        for z in range(max(lo + 1, lo if reach_up else 0) if reach_up else 0, count + 1):
            at = start + z
            inside = jnp.where((at >= 0) & (at < NZ), 1.0, 0.0)
            value = sweep(n, jnp.clip(at, 0, NZ - 1), third[z], third.get(z - 1, zero), third[z + 1])
            fourth[z] = value * inside
        return [
            sweep(n, start + z, fourth[z], fourth.get(z - 1, zero), fourth[z + 1])
            for z in range(count)
        ]

    for n in range(NS):
        top[n] = window(n, jnp.int32(0), False, 1)[0]

    row0 = (me_s * (C * W)) // HX
    for r in range(R):
        for c in range(3):
            total = None
            for n in range(NS):
                re = top[n, c, pl.ds(row0 + r, 1), :]
                im = top[n, c + 3, pl.ds(row0 + r, 1), :]
                part = factors[n][0] * re - factors[n][1] * im
                total = part if total is None else total + part
            sbuf[r, c] = total

    def surf_copy(k):
        to = lax.rem(me_c + k, C)
        return pltpu.make_async_remote_copy(
            sbuf.at[(to * W) // HX if R > 1 else 0], rbuf.at[k - 1],
            surf_send.at[k], surf_recv.at[k],
            device_id={"contour": to}, device_id_type=MESH,
        )

    surf_sends = [surf_copy(k) for k in range(1, C)]
    for copy in surf_sends:
        copy.start()

    def finish(n, carry):
        for z, value in enumerate(window(n, me_s * D, True, D)):
            for c in range(6):
                field_ref[n, c, pl.ds(z, HY, stride=D), :] = value[c]
        return carry

    lax.fori_loop(0, NS, finish, 0)

    for copy in surf_sends:
        copy.wait_recv()
    total = sbuf[(me_c * W) // HX if R > 1 else 0]
    for k in range(1, C):
        total = total + rbuf[k - 1]
    offset = lax.rem((me_s * C + me_c) * W, HX)
    surf_ref[...] = pltpu.roll(total, lax.rem(HX - offset, HX), 2)

    for copy in surf_sends:
        copy.wait_send()
    for pair in sends:
        for copy in pair:
            copy.wait_send()


def per_device(
    body_force, ice_thickness, ice_mask, layer_ids, shear_modulus, relax_rate, node_ids, time_ids
):
    S, C = lax.axis_size("space"), lax.axis_size("contour")
    NS, L, D, NT = node_ids.shape[0], shear_modulus.shape[0], layer_ids.shape[0], time_ids.shape[0]
    NZ = S * D
    NCZ = NZ // 2
    NJ = NCZ // 4
    W = HX * HY // (S * C)
    R = max(1, C * W // HX)
    NTP = -(-NT // 8) * 8
    body = body_force.reshape(3, D, HY, HX).transpose(0, 2, 1, 3).reshape(3, HY * D, HX)
    layers = layer_ids.reshape(D, HY, HX).transpose(1, 0, 2).reshape(HY * D, HX)
    tile = (HY, HX)
    vmem = pl.BlockSpec(memory_space=pltpu.VMEM)
    field, surf = pl.pallas_call(
        functools.partial(kernel, S, C, NS, L, D, NT, W),
        out_shape=(
            jax.ShapeDtypeStruct((NS, 6, HY * D, HX), F32),
            jax.ShapeDtypeStruct((3, NTP, HX), F32),
        ),
        in_specs=[pl.BlockSpec(memory_space=pltpu.HBM)] * 8,
        out_specs=(vmem, vmem),
        scratch_shapes=[
            pltpu.VMEM(tile, F32),
            pltpu.VMEM(tile, jnp.int32),
            pltpu.SMEM((L,), F32),
            pltpu.SMEM((L,), F32),
            pltpu.SMEM((NS,), jnp.int32),
            pltpu.SMEM((NT,), jnp.int32),
            pltpu.SemaphoreType.DMA((8,)),
            pltpu.VMEM((S, 3, HY * D, HX), F32),
            pltpu.VMEM((S, HY * D, HX), jnp.int32),
            pltpu.VMEM((NS, L, 8) + tile, F32),
            pltpu.VMEM((NS, 2) + tile, F32),
            pltpu.VMEM((NS, NZ, 7) + tile, F32),
            pltpu.VMEM((NZ, 3) + tile, F32),
            pltpu.VMEM((NS, NZ + 4, 6) + tile, F32),
            pltpu.VMEM((NS, NZ + 4, 6) + tile, F32),
            pltpu.VMEM((NCZ, L - 1) + tile, F32),
            pltpu.VMEM((NS, NCZ, 6) + tile, F32),
            pltpu.VMEM((NS, NJ, 6) + tile, F32),
            pltpu.VMEM((NS, 6) + tile, F32),
            pltpu.VMEM((R, 3, NTP, HX), F32),
            pltpu.VMEM((C - 1, 3, NTP, HX), F32),
            pltpu.SemaphoreType.DMA((S,)),
            pltpu.SemaphoreType.DMA((S,)),
            pltpu.SemaphoreType.DMA((S,)),
            pltpu.SemaphoreType.DMA((S,)),
            pltpu.SemaphoreType.DMA((C,)),
            pltpu.SemaphoreType.DMA((C,)),
        ],
        compiler_params=pltpu.CompilerParams(
            collective_id=0, has_side_effects=True, vmem_limit_bytes=48 * 1024 * 1024
        ),
    )(
        body,
        ice_thickness.reshape(HY, HX),
        ice_mask.reshape(HY, HX),
        layers,
        shear_modulus,
        relax_rate,
        node_ids,
        time_ids,
    )
    field = field.reshape(NS, 6, HY, D, HX).transpose(0, 1, 3, 2, 4).reshape(NS, 6, D, HY * HX)
    surf = surf[:, :NT, :W].transpose(1, 0, 2)
    return (field, surf)


def solution(mesh):
    in_specs = (
        P("groups", "space", None),
        P("groups"),
        P("groups"),
        P("space", None),
        P(),
        P(),
        P("contour"),
        P("groups"),
    )
    out_specs = (
        P(("groups", "contour"), None, "space", None),
        P("groups", None, ("space", "contour")),
    )
    return jax.shard_map(
        per_device, mesh=mesh, in_specs=in_specs, out_specs=out_specs, check_vma=False
    )
```

```python
import functools
import math

import jax
import jax.numpy as jnp
from jax import lax
from jax.experimental import pallas as pl
from jax.experimental.pallas import tpu as pltpu
from jax.sharding import PartitionSpec as P

HX = 128
HY = 8
T_STEPS = 64
COARSE_SWEEPS = 8
OMEGA = 0.7
MESH = pl.DeviceIdType.MESH
F32 = jnp.float32


def poles(nodes, node_count):
    angles = -math.pi + (nodes + 0.5) * (2.0 * math.pi / node_count)
    scale = 0.5 * node_count
    sine = jnp.sin(angles)
    cot = jnp.cos(angles) / sine
    pole_r = scale * (0.5017 * angles * cot - 0.4622)
    pole_i = scale * 0.2645 * angles
    slope_r = scale * 0.5017 * (cot - angles / (sine * sine))
    weight_r = scale * 0.2645 / node_count
    weight_i = -slope_r / node_count
    return pole_r, pole_i, weight_r, weight_i


def iota(shape, axis):
    return lax.broadcasted_iota(jnp.int32, shape, len(shape) + axis)


def shift(v, lanes, rows):
    if lanes:
        v = pltpu.roll(v, lanes % HX, v.ndim - 1)
    if rows:
        v = pltpu.roll(v, rows % HY, v.ndim - 2)
    return v


def sides(v, step):
    lane, row = iota(v.shape, -1), iota(v.shape, -2)
    left = jnp.where(lane >= step, shift(v, step, 0), 0.0)
    right = jnp.where(lane < HX - step, shift(v, -step, 0), 0.0)
    front = jnp.where(row >= step, shift(v, 0, step), 0.0)
    back = jnp.where(row < HY - step, shift(v, 0, -step), 0.0)
    return (left + right) + (front + back)


def even_lane(shape):
    return iota(shape, -1) % 2 == 0


def even_row(shape):
    return iota(shape, -2) % 2 == 0


def partner_lane(v):
    return jnp.where(even_lane(v.shape), shift(v, -1, 0), shift(v, 1, 0))


def partner_row(v):
    return jnp.where(even_row(v.shape), shift(v, 0, -1), shift(v, 0, 1))


def pack(a0, a1, a2, a3):
    el, er = even_lane(a0.shape), even_row(a0.shape)
    h0 = jnp.where(el, a0, a1) + jnp.where(el, shift(a0, -1, 0), shift(a1, 1, 0))
    h1 = jnp.where(el, a2, a3) + jnp.where(el, shift(a2, -1, 0), shift(a3, 1, 0))
    return jnp.where(er, h0, h1) + jnp.where(er, shift(h0, 0, -1), shift(h1, 0, 1))


def next_slot(v):
    return jnp.where(
        even_lane(v.shape),
        shift(v, -1, 0),
        jnp.where(even_row(v.shape), shift(v, 1, -1), 0.0),
    )


def last_slot(v):
    return jnp.where(
        even_lane(v.shape),
        jnp.where(even_row(v.shape), 0.0, shift(v, -1, 1)),
        shift(v, 1, 0),
    )


def prolong(v, slot):
    v = jnp.where(iota(v.shape, -1) % 2 == slot % 2, v, partner_lane(v))
    return jnp.where(iota(v.shape, -2) % 2 == slot // 2, v, partner_row(v))


def scaled(real, imag, v):
    re, im = v[:3], v[3:]
    return jnp.concatenate([real * re - imag * im, real * im + imag * re], axis=0)


def kernel(
    S, C, NS, L, D, NT, W,
    body_in, thick_in, mask_in, layer_in, shear_in, relax_in, node_in, time_in,
    field_out, surf_ref,
    field_ref, field_sem, thick_ref, mask_ref, shear_ref, relax_ref, node_ref, time_ref, load_sem,
    body_all, layer_all, tab, inv, coef, base, u1, u2, cnt, rz, coarse, top, sbuf, rbuf,
    body_send, body_recv, layer_send, layer_recv, surf_send, surf_recv,
):
    NZ = S * D
    NCZ = NZ // 2
    NJ = NCZ // 4
    NTP = sbuf.shape[2]
    R = sbuf.shape[0]
    tile = (HY, HX)
    me_s = lax.axis_index("space")
    me_c = lax.axis_index("contour")

    barrier = pltpu.get_barrier_semaphore()
    for k in range(1, S):
        pl.semaphore_signal(
            barrier, inc=1, device_id={"space": lax.rem(me_s + k, S)}, device_id_type=MESH
        )
    for k in range(1, C):
        pl.semaphore_signal(
            barrier, inc=1, device_id={"contour": lax.rem(me_c + k, C)}, device_id_type=MESH
        )
    loads = [
        pltpu.make_async_copy(source, target, load_sem.at[i])
        for i, (source, target) in enumerate(
            (
                (layer_in, layer_all.at[me_s]),
                (body_in, body_all.at[me_s]),
                (node_in, node_ref),
                (shear_in, shear_ref),
                (relax_in, relax_ref),
                (time_in, time_ref),
                (thick_in, thick_ref),
                (mask_in, mask_ref),
            )
        )
    ]
    for copy in loads:
        copy.start()
    for copy in loads[:2]:
        copy.wait()
    pl.semaphore_wait(barrier, S + C - 2)

    def slab_copies(k):
        peer = {"space": lax.rem(me_s + k, S)}
        return (
            pltpu.make_async_remote_copy(
                layer_all.at[me_s], layer_all.at[me_s], layer_send.at[k], layer_recv.at[k],
                device_id=peer, device_id_type=MESH,
            ),
            pltpu.make_async_remote_copy(
                body_all.at[me_s], body_all.at[me_s], body_send.at[k], body_recv.at[k],
                device_id=peer, device_id_type=MESH,
            ),
        )

    sends = [slab_copies(k) for k in range(1, S)]
    for pair in sends:
        for copy in pair:
            copy.start()

    for copy in loads[2:]:
        copy.wait()

    node_vec = jnp.stack([jnp.full(tile, node_ref[n].astype(F32)) for n in range(NS)])
    pole_r, pole_i, weight_r, weight_i = poles(node_vec, NS * C)
    square = pole_r * pole_r + pole_i * pole_i
    inv_r, inv_i = pole_r / square, -pole_i / square
    for n in range(NS):
        inv[n, 0] = inv_r[n]
        inv[n, 1] = inv_i[n]
    for l in range(L):
        shear, relax = shear_ref[l], relax_ref[l]
        moved = pole_r + relax
        denom = moved * moved + pole_i * pole_i
        mu_r = shear * ((pole_r * moved + pole_i * pole_i) / denom)
        mu_i = shear * ((pole_i * moved - pole_r * pole_i) / denom)
        size = shear * jnp.sqrt(square / denom)
        diag_r, diag_i = 6.0 * mu_r + 1.0, 6.0 * mu_i
        bound = 6.0 * size + 1.0
        scale = OMEGA / (bound * bound)
        gain_r, gain_i = diag_r * scale, -diag_i * scale
        rows = (
            1.0 - scale * (diag_r * diag_r + diag_i * diag_i),
            gain_r * mu_r - gain_i * mu_i,
            gain_r * mu_i + gain_i * mu_r,
            gain_r * inv_r - gain_i * inv_i,
            gain_r * inv_i + gain_i * inv_r,
            mu_r,
            mu_i,
            size,
        )
        for q, value in enumerate(rows):
            for n in range(NS):
                tab[n, l, q] = value[n]

    spots = iota((NTP, HX), -2)
    times = jnp.zeros((NTP, HX), F32)
    for j in range(NT):
        times = jnp.where(spots == j, (time_ref[j].astype(F32) + 1.0) * (2.0 / T_STEPS), times)
    factors = []
    for n in range(NS):
        growth = jnp.exp(times * pole_r[n, :1, :])
        phase = times * pole_i[n, :1, :]
        cosine, sine = jnp.cos(phase), jnp.sin(phase)
        wi = weight_i[n, :1, :]
        factors.append(
            (growth * (weight_r * cosine - wi * sine), growth * (weight_r * sine + wi * cosine))
        )

    blank = jnp.zeros((NS, 2, 6) + tile, F32)
    for u in (u1, u2):
        u[:, pl.ds(0, 2)] = blank
        u[:, pl.ds(NZ + 2, 2)] = blank

    ice = thick_ref[...] * mask_ref[...].astype(F32)

    def take_slab(slab):
        for zp in range(D // 2):
            counts = None
            for z in (2 * zp, 2 * zp + 1):
                at = slab * D + z
                ids = layer_all[slab, pl.ds(z, HY, stride=D), :]
                force = jnp.stack(
                    [body_all[slab, c, pl.ds(z, HY, stride=D), :] for c in range(3)]
                )
                if z == 0:
                    load = jnp.where(slab == 0, ice, jnp.zeros_like(ice))
                    force = jnp.concatenate([(force[0] - load)[None], force[1:]], axis=0)
                base[at] = force
                one = [jnp.where(ids == l, 1.0, 0.0) for l in range(1, L)]
                counts = one if counts is None else [a + b for a, b in zip(counts, one)]
                wide = jnp.broadcast_to(ids[None], (7,) + tile)
                for n in range(NS):
                    value = tab[n, 0, pl.ds(0, 7)]
                    for l in range(1, L):
                        value = jnp.where(wide == l, tab[n, l, pl.ds(0, 7)], value)
                    coef[n, at] = value
                    u1[n, at + 2] = jnp.concatenate(
                        [value[3][None] * force, value[4][None] * force], axis=0
                    )
            for l in range(L - 1):
                cnt[slab * (D // 2) + zp, l] = counts[l]

    take_slab(me_s)

    def arrive(k, carry):
        for copy in slab_copies(k):
            copy.wait_recv()
        take_slab(lax.rem(me_s - k + S, S))
        return carry

    lax.fori_loop(1, S, arrive, 0)

    def sweep(n, at, v, below, above):
        co = coef[n, at]
        around = below + above + sides(v, 1)
        return u1[n, at + 2] + co[0][None] * v + scaled(co[1][None], co[2][None], around)

    def second(z, carry):
        for n in range(NS):
            u2[n, z + 2] = sweep(n, z, u1[n, z + 2], u1[n, z + 1], u1[n, z + 3])
        return carry

    lax.fori_loop(0, NZ, second, 0, unroll=4)

    def residual(zc, carry):
        for n in range(NS):
            total = None
            for z in (2 * zc, 2 * zc + 1):
                mu_r, mu_i = coef[n, z, 5][None], coef[n, z, 6][None]
                force = base[z]
                v = u2[n, z + 2]
                lap = u2[n, z + 1] + u2[n, z + 3] + sides(v, 1) - 6.0 * v
                right = jnp.concatenate([inv[n, 0][None] * force, inv[n, 1][None] * force], axis=0)
                r = right - v + scaled(mu_r, mu_i, lap)
                total = r if total is None else total + r
            rz[n, zc] = total
        return carry

    lax.fori_loop(0, NCZ, residual, 0, unroll=2)

    counts = [pack(*[cnt[q * NJ + j] for q in range(4)]) * 0.125 for j in range(NJ)]

    def prepare(n):
        rhs, first, dd, hr, hi, mr, mi = [], [], [], [], [], [], []
        for j in range(NJ):
            share = [counts[j][l] for l in range(L - 1)]
            rest = 1.0 - sum(share[1:], share[0])
            mixed = []
            for q in (5, 6, 7):
                value = rest * tab[n, 0, q]
                for l in range(1, L):
                    value = value + share[l - 1] * tab[n, l, q]
                mixed.append(value)
            mu_r, mu_i, size = mixed
            diag_r, diag_i = 1.5 * mu_r + 1.0, 1.5 * mu_i
            bound = 1.5 * size + 1.0
            scale = OMEGA / (bound * bound)
            gain_r, gain_i = diag_r * scale, -diag_i * scale
            mu_r, mu_i = 0.25 * mu_r, 0.25 * mu_i
            b = pack(*[rz[n, q * NJ + j] for q in range(4)]) * 0.125
            rhs.append(b)
            first.append(scaled(gain_r[None], gain_i[None], b))
            dd.append((1.0 - scale * (diag_r * diag_r + diag_i * diag_i))[None])
            hr.append((gain_r * mu_r - gain_i * mu_i)[None])
            hi.append((gain_r * mu_i + gain_i * mu_r)[None])
            mr.append(mu_r[None])
            mi.append(mu_i[None])
        return rhs, first, dd, hr, hi, mr, mi

    def around(e):
        out = []
        for j in range(NJ):
            above = e[j + 1] if j < NJ - 1 else next_slot(e[0])
            below = e[j - 1] if j > 0 else last_slot(e[NJ - 1])
            out.append(above + below + sides(e[j], 2))
        return out

    plans = [prepare(n) for n in range(NS)]

    def step(counter, states):
        new = []
        for n in range(NS):
            rhs, first, dd, hr, hi, mr, mi = plans[n]
            e = states[n]
            near = around(e)
            new.append(
                tuple(first[j] + dd[j] * e[j] + scaled(hr[j], hi[j], near[j]) for j in range(NJ))
            )
        return tuple(new)

    states = lax.fori_loop(
        0, COARSE_SWEEPS - 1, step, tuple(tuple(plans[n][1]) for n in range(NS))
    )
    for n in range(NS):
        rhs, first, dd, hr, hi, mr, mi = plans[n]
        e = states[n]
        near = around(e)
        left = None
        for j in range(NJ):
            part = rhs[j] - e[j] + scaled(mr[j], mi[j], near[j] - 6.0 * e[j])
            left = part if left is None else left + part
        left = left + partner_lane(left)
        left = (left + partner_row(left)) * (1.0 / NCZ)
        for j in range(NJ):
            coarse[n, j] = e[j] + left

    def window(n, start, reach_up, count):
        lo = -2 if reach_up else 0
        third = {}
        for z in range(lo, count + 2, 2):
            zc = start // 2 + z // 2
            inside = jnp.where((zc >= 0) & (zc < NCZ), 1.0, 0.0)
            at = jnp.clip(zc, 0, NCZ - 1)
            e = prolong(coarse[n, at % NJ], at // NJ) * inside
            for zz in (z, z + 1):
                if zz < count + 2:
                    third[zz] = u2[n, start + zz + 2] + e
        zero = jnp.zeros((6,) + tile, F32)
        fourth = {}
        for z in range(max(lo + 1, lo if reach_up else 0) if reach_up else 0, count + 1):
            at = start + z
            inside = jnp.where((at >= 0) & (at < NZ), 1.0, 0.0)
            value = sweep(n, jnp.clip(at, 0, NZ - 1), third[z], third.get(z - 1, zero), third[z + 1])
            fourth[z] = value * inside
        return [
            sweep(n, start + z, fourth[z], fourth.get(z - 1, zero), fourth[z + 1])
            for z in range(count)
        ]

    for n in range(NS):
        top[n] = window(n, jnp.int32(0), False, 1)[0]

    row0 = (me_s * (C * W)) // HX
    for r in range(R):
        for c in range(3):
            total = None
            for n in range(NS):
                re = top[n, c, pl.ds(row0 + r, 1), :]
                im = top[n, c + 3, pl.ds(row0 + r, 1), :]
                part = factors[n][0] * re - factors[n][1] * im
                total = part if total is None else total + part
            sbuf[r, c] = total

    def surf_copy(k):
        to = lax.rem(me_c + k, C)
        return pltpu.make_async_remote_copy(
            sbuf.at[(to * W) // HX if R > 1 else 0], rbuf.at[k - 1],
            surf_send.at[k], surf_recv.at[k],
            device_id={"contour": to}, device_id_type=MESH,
        )

    surf_sends = [surf_copy(k) for k in range(1, C)]
    for copy in surf_sends:
        copy.start()

    def field_copy(n):
        return pltpu.make_async_copy(field_ref.at[n], field_out.at[n], field_sem.at[n])

    def finish(n, carry):
        for z, value in enumerate(window(n, me_s * D, True, D)):
            for c in range(6):
                field_ref[n, c, pl.ds(z, HY, stride=D), :] = value[c]
        field_copy(n).start()
        return carry

    lax.fori_loop(0, NS, finish, 0)

    for copy in surf_sends:
        copy.wait_recv()
    total = sbuf[(me_c * W) // HX if R > 1 else 0]
    for k in range(1, C):
        total = total + rbuf[k - 1]
    offset = lax.rem((me_s * C + me_c) * W, HX)
    surf_ref[...] = pltpu.roll(total, lax.rem(HX - offset, HX), 2)

    for n in range(NS):
        field_copy(n).wait()
    for copy in surf_sends:
        copy.wait_send()
    for pair in sends:
        for copy in pair:
            copy.wait_send()


def per_device(
    body_force, ice_thickness, ice_mask, layer_ids, shear_modulus, relax_rate, node_ids, time_ids
):
    S, C = lax.axis_size("space"), lax.axis_size("contour")
    NS, L, D, NT = node_ids.shape[0], shear_modulus.shape[0], layer_ids.shape[0], time_ids.shape[0]
    NZ = S * D
    NCZ = NZ // 2
    NJ = NCZ // 4
    W = HX * HY // (S * C)
    R = max(1, C * W // HX)
    NTP = -(-NT // 8) * 8
    body = body_force.reshape(3, D, HY, HX).transpose(0, 2, 1, 3).reshape(3, HY * D, HX)
    layers = layer_ids.reshape(D, HY, HX).transpose(1, 0, 2).reshape(HY * D, HX)
    tile = (HY, HX)
    vmem = pl.BlockSpec(memory_space=pltpu.VMEM)
    field, surf = pl.pallas_call(
        functools.partial(kernel, S, C, NS, L, D, NT, W),
        out_shape=(
            jax.ShapeDtypeStruct((NS, 6, HY * D, HX), F32),
            jax.ShapeDtypeStruct((3, NTP, HX), F32),
        ),
        in_specs=[pl.BlockSpec(memory_space=pltpu.HBM)] * 8,
        out_specs=(pl.BlockSpec(memory_space=pltpu.HBM), vmem),
        scratch_shapes=[
            pltpu.VMEM((NS, 6, HY * D, HX), F32),
            pltpu.SemaphoreType.DMA((NS,)),
            pltpu.VMEM(tile, F32),
            pltpu.VMEM(tile, jnp.int32),
            pltpu.SMEM((L,), F32),
            pltpu.SMEM((L,), F32),
            pltpu.SMEM((NS,), jnp.int32),
            pltpu.SMEM((NT,), jnp.int32),
            pltpu.SemaphoreType.DMA((8,)),
            pltpu.VMEM((S, 3, HY * D, HX), F32),
            pltpu.VMEM((S, HY * D, HX), jnp.int32),
            pltpu.VMEM((NS, L, 8) + tile, F32),
            pltpu.VMEM((NS, 2) + tile, F32),
            pltpu.VMEM((NS, NZ, 7) + tile, F32),
            pltpu.VMEM((NZ, 3) + tile, F32),
            pltpu.VMEM((NS, NZ + 4, 6) + tile, F32),
            pltpu.VMEM((NS, NZ + 4, 6) + tile, F32),
            pltpu.VMEM((NCZ, L - 1) + tile, F32),
            pltpu.VMEM((NS, NCZ, 6) + tile, F32),
            pltpu.VMEM((NS, NJ, 6) + tile, F32),
            pltpu.VMEM((NS, 6) + tile, F32),
            pltpu.VMEM((R, 3, NTP, HX), F32),
            pltpu.VMEM((C - 1, 3, NTP, HX), F32),
            pltpu.SemaphoreType.DMA((S,)),
            pltpu.SemaphoreType.DMA((S,)),
            pltpu.SemaphoreType.DMA((S,)),
            pltpu.SemaphoreType.DMA((S,)),
            pltpu.SemaphoreType.DMA((C,)),
            pltpu.SemaphoreType.DMA((C,)),
        ],
        compiler_params=pltpu.CompilerParams(
            collective_id=0, has_side_effects=True, vmem_limit_bytes=60 * 1024 * 1024
        ),
    )(
        body,
        ice_thickness.reshape(HY, HX),
        ice_mask.reshape(HY, HX),
        layers,
        shear_modulus,
        relax_rate,
        node_ids,
        time_ids,
    )
    field = field.reshape(NS, 6, HY, D, HX).transpose(0, 1, 3, 2, 4).reshape(NS, 6, D, HY * HX)
    surf = surf[:, :NT, :W].transpose(1, 0, 2)
    return (field, surf)


def solution(mesh):
    in_specs = (
        P("groups", "space", None),
        P("groups"),
        P("groups"),
        P("space", None),
        P(),
        P(),
        P("contour"),
        P("groups"),
    )
    out_specs = (
        P(("groups", "contour"), None, "space", None),
        P("groups", None, ("space", "contour")),
    )
    return jax.shard_map(
        per_device, mesh=mesh, in_specs=in_specs, out_specs=out_specs, check_vma=False
    )
```
